256 devices in a mesh: slab: 4 (over x_lo, core), kt: 64 (over z, y, x_hi).
Axes of the slice: x: 4 (x_hi: 2, x_lo: 2; x = x_hi * 2 + x_lo), y: 4, z: 8, core: 2. Of those that a mesh axis runs over, the one named last changes fastest.
Arguments:
- energies: float32 [4], replicated, may hold values from -0.5 to 0.1
- onsite: float32 [64, 4, 384], P('kt', 'slab'), may hold values from -3.5 to -2.5
- hamiltonian: bfloat16 [64, 4, 2, 384, 384], P('kt', 'slab'), may hold values from -0.109375 to 0.109375
- hopping: bfloat16 [64, 4, 2, 384, 384], P('kt', 'slab'), may hold values from -0.15625 to 0.15625
- contact: bfloat16 [64, 2, 384, 384], P('kt'), may hold values from -2 to 2
- previous: bfloat16 [64, 4, 4, 2, 2, 384, 384], P('kt', None, 'slab'), may hold values from -4 to 4
- neighbours: int32 [64, 2], P('kt'), may hold values from 0 to 63, as said below
- mode_index: int32 [64, 2], P('kt'), may hold values from 0 to 3
- mode_strength: float32 [4], replicated, may hold values from 0.25 to 1
Outputs:
- retarded: bfloat16 [64, 4, 4, 2, 384, 384], P('kt', None, 'slab')
- lesser: bfloat16 [64, 4, 4, 2, 384, 384], P('kt', None, 'slab')
The draws below stay inside these ranges and needn't reach their ends.
Inputs may be any that keep to these rules, and one draw needn't show every extreme that they name: neighbours[k, 0] is k - 1 or k - 2 and neighbours[k, 1] is k + 1 or k + 2, modulo 64.
All inputs are finite; a program needn't handle non-finite values.
Results may differ from the reference program's by a relative error of at most 0.017.
Values may be sent and summed in bfloat16 or wider, within the bound.
No kernel may reach another device: no remote copies, remote signals or barrier semaphores. Data moves between devices by JAX's collectives and lax.ppermute only.
A program may use at most 128 MiB of HBM per device.

```python
import math
import jax
import jax.numpy as jnp
from jax import lax

B = 384
NE = 4
MODES = 4
NSL = 4
K = 64


def draw_previous(key, part):
    full_shape = (K, NE, NSL, 2, 2, B, B)
    values = jax.random.truncated_normal(key, -4.0, 4.0, full_shape, jnp.float32)
    kinds = jnp.arange(2).reshape(1, 1, 1, 2, 1, 1, 1)
    factor = jnp.where(kinds == 0, 1.0 / math.sqrt(B), 1.0)
    return (values * factor).astype(jnp.bfloat16)


def draw_contact(key, part):
    full_shape = (K, 2, B, B)
    key_off = jax.random.fold_in(key, 11)
    key_real = jax.random.fold_in(key, 12)
    key_imag = jax.random.fold_in(key, 13)
    spread = jax.random.truncated_normal(key_off, -4.0, 4.0, full_shape, jnp.float32)
    level_real = jax.random.uniform(key_real, (K, B), jnp.float32, -0.3, 0.3)
    level_imag = jnp.exp(jax.random.uniform(key_imag, (K, B), jnp.float32, math.log(0.5), math.log(1.5)))
    identity = jnp.eye(B, dtype=jnp.float32)
    diagonal_part = jnp.stack([level_real[:, :, None] * identity[None], -level_imag[:, :, None] * identity[None]], axis=1)
    values = spread * (0.5 / math.sqrt(B)) + diagonal_part
    return values.astype(jnp.bfloat16)


def draw_neighbours(key, part):
    distance = jax.random.randint(key, (K, 2), 1, 3)
    kpoints = jnp.arange(K)
    backward = (kpoints - distance[:, 0]) % K
    forward = (kpoints + distance[:, 1]) % K
    return jnp.stack([backward, forward], axis=1).astype(jnp.int32)


def touch_ends(drawn, rng, smallest, top_value):
    shape = drawn.shape
    place = [jax.random.randint(jax.random.fold_in(rng, axis), (), 0, shape[axis]) for axis in range(len(shape))]
    drawn = drawn.at[tuple(place)].set(smallest)
    longest = shape.index(max(shape))
    place[longest] = (place[longest] + 1) % shape[longest]
    return drawn.at[tuple(place)].set(top_value)


def steps_of(stream_key, shape, split, smallest, largest):
    def one(position, blocks):
        draws = jax.random.uniform(jax.random.fold_in(jax.random.fold_in(stream_key, 6), position), (blocks,), jnp.float32, smallest / len(split), largest / len(split))
        return jnp.repeat(jnp.exp(draws), shape[position] // blocks).reshape((-1,) + (1,) * (len(shape) - position - 1))

    factor_of = one(*split[0])
    for cut in split[1:]:
        factor_of = factor_of * one(*cut)
    return factor_of


def noise(key, extent, width, reach, cuts=(), kind=jnp.bfloat16):
    gain = steps_of(key, extent, cuts, -0.22, 0.18) if cuts else 1.0
    values = jax.random.normal(key, extent, jnp.float32) * width * gain
    return jnp.minimum(jnp.maximum(values, -reach), reach).astype(kind)


def setup_inputs(seed: int = 0) -> dict:
    key_of = jax.random.split(jax.random.key(seed), 10)
    return {
        "energies": jnp.clip(jax.random.uniform(key_of[0], (NE,), jnp.float32, -0.5, 0.1), -0.5, 0.1),
        "onsite": jnp.clip(-3.5 + 1.0 * jax.random.uniform(key_of[1], (K, NSL, B), jnp.float32) ** steps_of(key_of[1], (K, NSL, B), ((0, 64), (1, 4)), -0.2, 0.2), -3.5, -2.5),
        "hamiltonian": noise(key_of[2], (K, NSL, 2, B, B), (8 * B) ** -0.5, 0.109375, ((0, 64), (1, 4))),
        "hopping": noise(key_of[3], (K, NSL, 2, B, B), (4 * B) ** -0.5, 0.15625, ((0, 64), (1, 4))),
        "contact": draw_contact(jax.random.fold_in(key_of[9], 71), 0),
        "previous": draw_previous(jax.random.fold_in(key_of[9], 71), 0),
        "neighbours": draw_neighbours(jax.random.fold_in(key_of[9], 71), 0),
        "mode_index": touch_ends(jax.random.randint(key_of[7], (K, 2), 0, MODES), jax.random.fold_in(key_of[7], 1), 0, MODES - 1).astype(jnp.int32),
        "mode_strength": jnp.clip(jnp.exp(jax.random.uniform(key_of[8], (MODES,), jnp.float32, math.log(0.25), math.log(1.0))), 0.25, 1.0),
    }


broaden = 0.05
fermi_level = 0.0
thermal = 0.1


def complex_mul(first_op, second_op):
    real_real = jnp.dot(first_op[0], second_op[0], preferred_element_type=jnp.float32)
    imag_imag = jnp.dot(first_op[1], second_op[1], preferred_element_type=jnp.float32)
    real_imag = jnp.dot(first_op[0], second_op[1], preferred_element_type=jnp.float32)
    imag_real = jnp.dot(first_op[1], second_op[0], preferred_element_type=jnp.float32)
    return jnp.stack([real_real - imag_imag, real_imag + imag_real])


def adjoint(matrix):
    return jnp.stack([matrix[0].T, -matrix[1].T])


def slab_update(boundary, energy, levels, hamilton, coupling, phonon):
    conjugate = adjoint(coupling)
    moved_r = complex_mul(coupling, boundary[0]).astype(jnp.bfloat16)
    moved_l = complex_mul(coupling, boundary[1]).astype(jnp.bfloat16)
    self_retarded = complex_mul(moved_r, conjugate)
    self_lesser = complex_mul(moved_l, conjugate)
    identity = jnp.eye(levels.shape[0], dtype=jnp.float32)
    system_real = (energy - levels)[:, None] * identity - hamilton[0].astype(jnp.float32) - self_retarded[0] - phonon[0, 0]
    system_imaginary = broaden * identity - hamilton[1].astype(jnp.float32) - self_retarded[1] - phonon[0, 1]
    diagonal_real = jnp.diagonal(system_real)
    diagonal_imaginary = jnp.diagonal(system_imaginary)
    modulus = diagonal_real * diagonal_real + diagonal_imaginary * diagonal_imaginary
    inverse_real = diagonal_real / modulus
    inverse_imaginary = -diagonal_imaginary / modulus
    scaled_real = inverse_real[:, None] * system_real - inverse_imaginary[:, None] * system_imaginary
    scaled_imaginary = inverse_real[:, None] * system_imaginary + inverse_imaginary[:, None] * system_real
    sandwich_real = scaled_real * inverse_real[None, :] - scaled_imaginary * inverse_imaginary[None, :]
    sandwich_imaginary = scaled_real * inverse_imaginary[None, :] + scaled_imaginary * inverse_real[None, :]
    first_guess = jnp.stack([2.0 * jnp.diag(inverse_real) - sandwich_real, 2.0 * jnp.diag(inverse_imaginary) - sandwich_imaginary])
    first_rounded = first_guess.astype(jnp.bfloat16)
    system_rounded = jnp.stack([system_real, system_imaginary]).astype(jnp.bfloat16)
    product = complex_mul(system_rounded, first_rounded).astype(jnp.bfloat16)
    retarded = (2.0 * first_guess - complex_mul(first_rounded, product)).astype(jnp.bfloat16)
    source = (phonon[1] + self_lesser).astype(jnp.bfloat16)
    halfway = complex_mul(retarded, source).astype(jnp.bfloat16)
    lesser = complex_mul(halfway, adjoint(retarded)).astype(jnp.bfloat16)
    return retarded, lesser


def reference(energies, onsite, hamiltonian, hopping, contact, previous, neighbours, mode_index, mode_strength):
    points = neighbours.shape[0]
    slab_count = onsite.shape[1]

    def one_point(kpoint):
        neighbour_pair = neighbours[kpoint]
        chosen = mode_index[kpoint]
        strength = mode_strength[chosen]
        phonon = strength[0] * previous[neighbour_pair[0]].astype(jnp.float32) + strength[1] * previous[neighbour_pair[1]].astype(jnp.float32)
        contact_block = contact[kpoint]
        contact_float = contact_block.astype(jnp.float32)
        skew_part = jnp.stack([contact_float[0] - contact_float[0].T, contact_float[1] + contact_float[1].T])

        def one_energy(energy, phonon_energy):
            occupation = 1.0 / (1.0 + jnp.exp((energy - fermi_level) / thermal))
            boundary = jnp.stack([contact_block, (-occupation * skew_part).astype(jnp.bfloat16)])
            retarded_list = [None] * slab_count
            lesser_list = [None] * slab_count
            for slab_num in reversed(range(slab_count)):
                ret_block, les_block = slab_update(boundary, energy, onsite[kpoint, slab_num], hamiltonian[kpoint, slab_num], hopping[kpoint, slab_num], phonon_energy[slab_num])
                retarded_list[slab_num] = ret_block
                lesser_list[slab_num] = les_block
                boundary = jnp.stack([ret_block, les_block])
            return jnp.stack(retarded_list), jnp.stack(lesser_list)

        return jax.vmap(one_energy)(energies, phonon)

    retarded, lesser = lax.map(one_point, jnp.arange(points, dtype=jnp.int32))
    return retarded, lesser
```

```python
import functools

import jax
import jax.numpy as jnp
from jax import lax
from jax.experimental import pallas as pl
from jax.experimental.pallas import tpu as pltpu
from jax.sharding import PartitionSpec as P

broaden = 0.05
fermi_level = 0.0
thermal = 0.1

BF = jnp.bfloat16
F32 = jnp.float32
ANY = pl.BlockSpec(memory_space=pl.ANY)
SMEM = pl.BlockSpec(memory_space=pltpu.SMEM)
VMEM = pl.BlockSpec(memory_space=pltpu.VMEM)

A_SWAP, A_BEHIND, A_AHEAD = 0, 1, 2
B_BEHIND, B_AHEAD, B_SWAP = 3, 4, 5
EVEN = 6
ENERGY = 7
I_POS = 0
INFO = 16
NEAR_BEHIND, NEAR_AHEAD, MODE_BEHIND, MODE_AHEAD = 0, 1, 2, 3


def dot(a, b):
    return jnp.dot(a, b, preferred_element_type=F32)


def dot_nt(a, b):
    return lax.dot_general(a, b, (((1,), (1,)), ((), ())), preferred_element_type=F32)


def params(flops, nbytes):
    return dict(
        compiler_params=pltpu.CompilerParams(vmem_limit_bytes=24 * 1024 * 1024),
        cost_estimate=pl.CostEstimate(flops=flops, bytes_accessed=nbytes, transcendentals=0),
    )


def lay_out_kernel(blocks, with_info, n_dep, prev, *rest):
    info = rest[0] if with_info else None
    rest = rest[with_info + n_dep :]
    outs, buffers, sems = rest[: len(blocks)], rest[len(blocks) : 2 * len(blocks)], rest[-1]
    rows = prev.shape[2]
    loads, stores = [], []
    for i, (first, count, kind) in enumerate(blocks):
        loads.append(
            [
                pltpu.make_async_copy(
                    prev.at[first + e, kind], buffers[i].at[pl.ds(e * rows, rows)], sems.at[i, e]
                )
                for e in range(count)
            ]
        )
        for c in loads[-1]:
            c.start()
    for i, (first, count, kind) in enumerate(blocks):
        if with_info:
            buffers[i][count * rows :] = info[...]
        for c in loads[i]:
            c.wait()
        stores.append(pltpu.make_async_copy(buffers[i], outs[i], sems.at[i, 0]))
        stores[-1].start()
    for c in stores:
        c.wait()


def lay_out(n, number, blocks, prev, info, deps):
    shapes = [(b[1] * 2 * n + (0 if info is None else INFO), n) for b in blocks]
    most = max(b[1] for b in blocks)
    infos = [] if info is None else [info]
    return pl.pallas_call(
        functools.partial(lay_out_kernel, blocks, len(infos), len(deps)),
        out_shape=[jax.ShapeDtypeStruct(s, BF) for s in shapes],
        in_specs=[ANY] + [VMEM] * len(infos) + [ANY] * len(deps),
        out_specs=[ANY] * len(blocks),
        scratch_shapes=[pltpu.VMEM(s, BF) for s in shapes] + [pltpu.SemaphoreType.DMA((len(blocks), most))],
        name=f"lay_out_{number}",
        compiler_params=pltpu.CompilerParams(vmem_limit_bytes=60 * 1024 * 1024),
    )(prev, *infos, *deps)


def exchange_kernel(own_a, own_b, ne, modes, n_dep, fvec, prev, swapped, behind, ahead, info_s, info_b, info_a, *rest):
    up, down, mixed, own_v, beh_v, ahe_v, up_v, down_v, mix_v, info_v, sems = rest[n_dep:]
    rows = prev.shape[2]
    infos = []
    for i, r in enumerate((info_s, info_b, info_a)):
        c = pltpu.make_async_copy(r.at[pl.ds(r.shape[0] - INFO, INFO)], info_v.at[i], sems.at[7 + i])
        c.start()
        infos.append(c)
    loads = [
        pltpu.make_async_copy(prev.at[own_b[0] + e, own_b[2]], own_v.at[pl.ds(e * rows, rows)], sems.at[2])
        for e in range(own_b[1])
    ]
    loads += [
        pltpu.make_async_copy(r.at[pl.ds(0, own_b[1] * rows)], v, sems.at[3 + i])
        for i, (r, v) in enumerate(((behind, beh_v), (ahead, ahe_v)))
    ]
    for c in infos:
        c.wait()
    told = [info_v[i].astype(F32) for i in range(3)]

    def value(who, row):
        return jnp.max(told[who][row : row + 1, :])

    even = fvec[EVEN]
    take_up = even * value(2, NEAR_BEHIND)
    take_down = (1.0 - even) * value(1, NEAR_AHEAD)
    chosen = []
    for i, (flag, v, dst) in enumerate(((take_up, up_v, up), (take_down, down_v, down))):

        @pl.when(flag < 0.5)
        def _(i=i, v=v):
            for e in range(own_a[1]):
                pltpu.make_async_copy(
                    prev.at[own_a[0] + e, own_a[2]], v.at[pl.ds(e * rows, rows)], sems.at[i]
                ).start()

        @pl.when(flag >= 0.5)
        def _(i=i, v=v):
            pltpu.make_async_copy(swapped.at[pl.ds(0, own_a[1] * rows)], v, sems.at[i]).start()

        chosen.append((pltpu.make_async_copy(v, v, sems.at[i]), pltpu.make_async_copy(v, dst, sems.at[5 + i])))
    for c in loads:
        c.start()

    def strength(row):
        mode = value(0, row)
        picked = jnp.float32(0.0)
        for m in range(modes):
            picked = jnp.where(jnp.abs(mode - m) < 0.5, fvec[ENERGY + ne + m], picked)
        return picked

    want_behind = value(0, NEAR_BEHIND) * strength(MODE_BEHIND)
    want_ahead = value(0, NEAR_AHEAD) * strength(MODE_AHEAD)
    own_w = even * want_behind + (1.0 - even) * want_ahead
    behind_w = (1.0 - even) * want_behind
    ahead_w = even * want_ahead
    for load, store in chosen:
        load.wait()
        store.start()
    for c in loads:
        c.wait()
    for e in range(own_b[1]):
        r = slice(e * rows, (e + 1) * rows)
        mix_v[r] = (
            own_w * own_v[r].astype(F32)
            + behind_w * beh_v[r].astype(F32)
            + ahead_w * ahe_v[r].astype(F32)
        ).astype(BF)
    last = pltpu.make_async_copy(mix_v, mixed, sems.at[2])
    last.start()
    for _, store in chosen:
        store.wait()
    last.wait()


def exchange(n, number, own_a, own_b, ne, modes, fvec, prev, swapped, behind, ahead, infos, deps):
    a = (own_a[1] * 2 * n, n)
    b = (own_b[1] * 2 * n, n)
    return pl.pallas_call(
        functools.partial(exchange_kernel, own_a, own_b, ne, modes, len(deps)),
        out_shape=[jax.ShapeDtypeStruct(s, BF) for s in (a, a, b)],
        in_specs=[SMEM] + [ANY] * (7 + len(deps)),
        out_specs=[ANY] * 3,
        scratch_shapes=[pltpu.VMEM(s, BF) for s in (b, b, b, a, a, b)]
        + [pltpu.VMEM((3, INFO, n), BF), pltpu.SemaphoreType.DMA((10,))],
        name=f"exchange_{number}",
        **params(6 * n * n, 14 * n * n * 2),
    )(fvec, prev, swapped, behind, ahead, *infos, *deps)


def contact_kernel(ne, n_dep, fvec, contact, *rest):
    out = rest[n_dep]
    n = out.shape[-1]
    cr, ci = contact[0].astype(F32), contact[1].astype(F32)
    skew_r, skew_i = cr - cr.T, ci + ci.T
    for e in range(ne):
        energy = jnp.full((1, n), fvec[ENERGY + e], F32)
        minus = -1.0 / (1.0 + jnp.exp((energy - fermi_level) / thermal))
        out[e, :n] = (minus * skew_r).astype(BF)
        out[e, n:] = (minus * skew_i).astype(BF)


def starting_lesser(n, ne, fvec, contact, deps):
    return pl.pallas_call(
        functools.partial(contact_kernel, ne, len(deps)),
        out_shape=jax.ShapeDtypeStruct((ne, 2 * n, n), BF),
        in_specs=[SMEM, VMEM] + [ANY] * len(deps),
        out_specs=VMEM,
        name="contact",
        **params(20 * n * n, 12 * n * n * 2),
    )(fvec, contact, *deps)


def lag_of(slab, slabs):
    return 2 * (slabs - 1 - slab)


def slot_map(slot, slabs, energies):
    found = [(s, slot - lag_of(s, slabs)) for s in range(slabs)]
    return [(s, e) for s, e in found if 0 <= e < energies]


def fetch(ivec, active, pieces):
    for s, _ in active:

        @pl.when(ivec[I_POS] == s)
        def _(s=s):
            for source, dst, sem in pieces:
                pltpu.make_async_copy(source(s), dst, sem).start()


def fill(ref, n, low=True):
    ref[n:, :n] = -ref[:n, n:]
    if low:
        ref[n:, n:] = ref[:n, :n]


def put(ref, n, real, imaginary):
    ref[:n, :n] = real
    ref[:n, n:] = imaginary
    ref[n:, :n] = -imaginary
    ref[n:, n:] = real


def moved_and_self(n, crep, xrep, moved_v):
    fill(crep, n)
    fill(xrep, n)
    moved_v[...] = dot(crep[:n, :], xrep[...]).astype(BF)
    return dot_nt(moved_v[...], crep[...])


def weights_of(kind_of_block):
    return (A_SWAP, A_BEHIND, A_AHEAD) if kind_of_block == "a" else (B_BEHIND, B_AHEAD, B_SWAP)


def pick_weights(ivec, fvec, active, where):
    picked = [jnp.float32(0.0)] * 3
    for s, e in active:
        names = weights_of(where[e][1])
        picked = [jnp.where(ivec[I_POS] == s, fvec[w], p) for w, p in zip(names, picked)]
    return picked


def unpack(refs, n_fixed, wants, sources, n_skip):
    refs = list(refs)
    fixed, at = refs[:n_fixed], n_fixed
    boundaries = []
    for want in wants:
        boundaries.append(refs[at] if want else None)
        at += want
    groups = {}
    for g in sources:
        groups[g] = refs[at : at + 3]
        at += 3
    at += n_skip
    return fixed, boundaries, groups, refs[at], refs[at + 1], refs[at + 2 :]


def retarded_kernel(n, active, where, top, wants, sources, n_skip, *refs):
    fixed, (recv, contact), groups, send, state, scratch = unpack(refs, 5, wants, sources, n_skip)
    ivec, fvec, onsite, coupling, hamilton_h = fixed
    (xrep, crep, h_v, p0_v, p1_v, p2_v, moved_v, first_v, sys_v, frep, prep, out_v, sems) = scratch
    energy_of = dict(active)
    working = functools.reduce(jnp.logical_or, [ivec[I_POS] == s for s, _ in active])

    def boundary(s):
        return contact if s == top else recv

    fetch(
        ivec,
        active,
        parts_of(n, boundary, xrep, sems, 0)
        + parts_of(n, lambda s: coupling, crep, sems, 2)
        + [(lambda s: hamilton_h, h_v, sems.at[4])]
        + phonon_of(n, groups, where, energy_of, (p0_v, p1_v, p2_v), sems, 5),
    )

    @pl.when(working)
    def _():
        def wait(dst, k):
            pltpu.make_async_copy(dst, dst, sems.at[k]).wait()

        energy = jnp.float32(0.0)
        for s, e in active:
            energy = jnp.where(ivec[I_POS] == s, fvec[ENERGY + e], energy)
        w0, w1, w2 = pick_weights(ivec, fvec, active, where)
        wait_parts(n, wait, crep, 2)
        wait_parts(n, wait, xrep, 0)
        selfs = moved_and_self(n, crep, xrep, moved_v)
        for k, v in enumerate((h_v, p0_v, p1_v, p2_v)):
            wait(v, 4 + k)
        taken = (
            w0 * p0_v[...].astype(F32) + w1 * p1_v[...].astype(F32) + w2 * p2_v[...].astype(F32)
        )
        taken = taken + h_v[...].astype(F32)
        row = lax.broadcasted_iota(jnp.int32, (n, n), 0)
        col = lax.broadcasted_iota(jnp.int32, (n, n), 1)
        eye = row == col
        levels = energy - onsite[...]
        zero = jnp.zeros((n, n), F32)
        sr = jnp.where(eye, jnp.broadcast_to(levels, (n, n)), zero) - taken[:n] - selfs[:, :n]
        si = jnp.where(eye, jnp.full((n, n), broaden, F32), zero) - taken[n:] - selfs[:, n:]
        sys_v[:, :n] = sr.astype(BF)
        sys_v[:, n:] = si.astype(BF)
        diag_r = jnp.where(eye, sr, zero)
        diag_i = jnp.where(eye, si, zero)

        def reciprocal(axis):
            dr = jnp.sum(diag_r, axis=axis, keepdims=True)
            di = jnp.sum(diag_i, axis=axis, keepdims=True)
            modulus = dr * dr + di * di
            return dr / modulus, -di / modulus

        cr, ci = reciprocal(1)
        rr, ri = reciprocal(0)
        tr = cr * sr - ci * si
        ti = cr * si + ci * sr
        fr = jnp.where(eye, 2.0 * cr, zero) - (tr * rr - ti * ri)
        fi = jnp.where(eye, 2.0 * ci, zero) - (tr * ri + ti * rr)
        first_v[:, :n] = fr
        first_v[:, n:] = fi
        frb, fib = fr.astype(BF), fi.astype(BF)
        put(frep, n, frb, fib)
        product = dot(sys_v[...], frep[...])
        put(prep, n, product[:, :n].astype(BF), product[:, n:].astype(BF))
        correction = dot(frep[:n, :], prep[...])
        out_v[:n] = (2.0 * first_v[:, :n] - correction[:, :n]).astype(BF)
        out_v[n:] = (2.0 * first_v[:, n:] - correction[:, n:]).astype(BF)
        pltpu.make_async_copy(out_v, send, sems.at[8]).start()

    for s, e in active:

        @pl.when(ivec[I_POS] == s)
        def _(e=e):
            pltpu.make_async_copy(out_v, state.at[e], sems.at[9]).start()

    @pl.when(working)
    def _():
        pltpu.make_async_copy(out_v, send, sems.at[8]).wait()
        pltpu.make_async_copy(out_v, send, sems.at[9]).wait()


def lesser_kernel(n, active, where, top, wants, sources, n_skip, *refs):
    fixed, (recv, contact), groups, send, state, scratch = unpack(refs, 4, wants, sources, n_skip)
    ivec, fvec, coupling, ret_h = fixed
    (xrep, crep, p0_v, p1_v, p2_v, moved_v, rrep, srep, half_v, out_v, sems) = scratch
    energy_of = dict(active)
    working = functools.reduce(jnp.logical_or, [ivec[I_POS] == s for s, _ in active])

    def boundary(s):
        return contact.at[energy_of[s]] if s == top else recv

    fetch(
        ivec,
        active,
        parts_of(n, boundary, xrep, sems, 0)
        + parts_of(n, lambda s: coupling, crep, sems, 2)
        + parts_of(n, lambda s: ret_h, rrep, sems, 4)
        + phonon_of(n, groups, where, energy_of, (p0_v, p1_v, p2_v), sems, 6),
    )

    @pl.when(working)
    def _():
        def wait(dst, k):
            pltpu.make_async_copy(dst, dst, sems.at[k]).wait()

        w0, w1, w2 = pick_weights(ivec, fvec, active, where)
        wait_parts(n, wait, crep, 2)
        wait_parts(n, wait, xrep, 0)
        selfs = moved_and_self(n, crep, xrep, moved_v)
        for k, v in enumerate((p0_v, p1_v, p2_v)):
            wait(v, 6 + k)
        taken = (
            w0 * p0_v[...].astype(F32) + w1 * p1_v[...].astype(F32) + w2 * p2_v[...].astype(F32)
        )
        put(srep, n, (taken[:n] + selfs[:, :n]).astype(BF), (taken[n:] + selfs[:, n:]).astype(BF))
        wait_parts(n, wait, rrep, 4)
        fill(rrep, n)
        half_v[...] = dot(rrep[:n, :], srep[...]).astype(BF)
        lesser = dot_nt(half_v[...], rrep[...])
        out_v[:n] = lesser[:, :n].astype(BF)
        out_v[n:] = lesser[:, n:].astype(BF)
        pltpu.make_async_copy(out_v, send, sems.at[9]).start()

    for s, e in active:

        @pl.when(ivec[I_POS] == s)
        def _(e=e):
            pltpu.make_async_copy(out_v, state.at[e], sems.at[10]).start()

    @pl.when(working)
    def _():
        pltpu.make_async_copy(out_v, send, sems.at[9]).wait()
        pltpu.make_async_copy(out_v, send, sems.at[10]).wait()


def parts_of(n, source, rep, sems, at):
    return [
        (lambda s: source(s).at[:n], rep.at[:n, :n], sems.at[at]),
        (lambda s: source(s).at[n:], rep.at[:n, n:], sems.at[at + 1]),
    ]


def wait_parts(n, wait, rep, at):
    wait(rep.at[:n, :n], at)
    wait(rep.at[:n, n:], at + 1)


def phonon_of(n, groups, where, energy_of, buffers, sems, at):
    def source(i):
        def found(s):
            pair, block, inside = where[energy_of[s]]
            return groups[pair, block][i].at[pl.ds(inside * 2 * n, 2 * n)]

        return found

    return [(source(i), v, sems.at[at + i]) for i, v in enumerate(buffers)]


def slab_call(kernel, name, n, slot, slabs, energies, where, scalars, fixed, recv, top_block, phonon, state, deps, scratch, flops):
    active = slot_map(slot, slabs, energies)
    top = slabs - 1
    wants = (
        any(s != top for s, _ in active),
        any(s == top for s, _ in active),
    )
    sources = sorted({where[e][:2] for _, e in active})
    operands = list(scalars) + list(fixed)
    n_vmem = len(scalars) - 2
    operands += [b for b, want in zip((recv, top_block), wants) if want]
    for g in sources:
        operands += list(phonon[g])
    aliases = {}
    if state is not None:
        aliases = {len(operands): 1}
        operands.append(state)
    operands += list(deps)
    block = jax.ShapeDtypeStruct((2 * n, n), BF)
    return pl.pallas_call(
        functools.partial(
            kernel, n, active, where, top, wants, sources, (state is not None) + len(deps)
        ),
        out_shape=[block, jax.ShapeDtypeStruct((energies, 2 * n, n), BF)],
        in_specs=[SMEM, SMEM] + [VMEM] * n_vmem + [ANY] * (len(operands) - 2 - n_vmem),
        out_specs=[ANY, ANY],
        scratch_shapes=scratch,
        input_output_aliases=aliases,
        name=f"{name}_{slot}",
        **params(flops * n * n * n, 20 * n * n * 2),
    )(*operands)


def retarded_scratch(n):
    b = pltpu.VMEM((2 * n, n), BF)
    w = pltpu.VMEM((2 * n, 2 * n), BF)
    t = pltpu.VMEM((n, 2 * n), BF)
    return [w, w, b, b, b, b, t, pltpu.VMEM((n, 2 * n), F32), t, w, w, b, pltpu.SemaphoreType.DMA((10,))]


def lesser_scratch(n):
    b = pltpu.VMEM((2 * n, n), BF)
    w = pltpu.VMEM((2 * n, 2 * n), BF)
    t = pltpu.VMEM((n, 2 * n), BF)
    return [w, w, b, b, b, t, w, w, t, b, pltpu.SemaphoreType.DMA((11,))]


def pairs_of(ne):
    half = ne // 2
    return [
        ((0, half, 0), (half, half, 0)),
        ((0, half, 1), (half, half, 1)),
    ]


PLAN = (
    "w0", "w1", "c", "x0", "x1", "d0b", "r0", "r1", "r2", "d1a", "d1b", "r3", "l0", "r4", "l1", "r5", "l2", "r6", "l3", "r7", "l4", "r8", "l5", "r9", "l6", "l7", "l8", "l9",
)


def body(energies, onsite, hamiltonian, hopping, contact, previous, neighbours, mode_index, mode_strength):
    slabs = lax.axis_size("slab")
    points = lax.axis_size("kt")
    pos = lax.axis_index("slab")
    k = lax.axis_index("kt")
    ne, n = previous.shape[1], previous.shape[-1]
    modes = mode_strength.shape[0]

    def along(value, shift):
        return lax.ppermute(value, "kt", [(i, (i + shift) % points) for i in range(points)])

    def swap(value):
        return lax.ppermute(value, "kt", [(i, i ^ 1) for i in range(points)])

    def hand_on(value, slot):
        senders = [s for s, _ in slot_map(slot, slabs, ne) if s > 0]
        return lax.ppermute(value, "slab", [(s, s - 1) for s in senders]) if senders else None

    pairs = pairs_of(ne)
    where = [{}, {}]
    for p, both in enumerate(pairs):
        for name, (first, count, kind) in zip("ab", both):
            for e in range(count):
                where[kind][first + e] = (p, name, e)
    prev = previous.reshape(ne, 2, 2 * n, n)

    strength = jnp.sum(
        jnp.where(mode_index[0][:, None] == jnp.arange(modes)[None, :], mode_strength[None, :], 0.0), axis=1
    )
    wanted = jnp.stack([(k - 1) % points, (k + 1) % points])
    near = (neighbours[0] == wanted).astype(F32)
    info = jnp.concatenate([near, mode_index[0].astype(F32), jnp.zeros((INFO - 4,), F32)])
    info = jnp.broadcast_to(info[:, None], (INFO, n)).astype(BF)
    even = (k % 2 == 0).astype(F32)
    odd = 1.0 - even
    far = 1.0 - near
    fvec = jnp.concatenate(
        [
            jnp.stack(
                [
                    even * near[1] * strength[1] + odd * near[0] * strength[0],
                    strength[0] * (even + odd * far[0]),
                    strength[1] * (odd + even * far[1]),
                    strength[0] * far[0],
                    strength[1] * far[1],
                    jnp.float32(1.0),
                    even,
                ]
            ),
            energies,
            mode_strength,
        ]
    )
    ivec = jnp.stack([pos, pos]).astype(jnp.int32)
    coupling = hopping.reshape(2 * n, n)
    hamilton = hamiltonian.reshape(2 * n, n)
    contact_r = contact.reshape(2 * n, n)
    contact_l = None
    levels = onsite.reshape(1, n)

    swapped, from_behind, from_ahead = {}, {}, {}
    phonon = {}
    slots = ne + lag_of(0, slabs)
    state = [None, None]
    handed = [{}, {}]
    ret_of = {}
    deps = []

    def do_lay_out(p):
        nonlocal deps
        block_a, block_b = lay_out(n, p, pairs[p], prev, info if p == 0 else None, deps)
        swapped[p] = swap(block_a)
        from_behind[p] = along(block_b, 2)
        from_ahead[p] = along(block_b, -2)
        deps = [block_b]

    def do_exchange(p):
        nonlocal deps
        own_a, own_b = pairs[p]
        up_block, down_block, mixed = exchange(
            n, p, own_a, own_b, ne, modes, fvec, prev, swapped[p], from_behind[p], from_ahead[p],
            (swapped[0], from_behind[0], from_ahead[0]), deps,
        )
        phonon[p, "a"] = (swapped[p], along(up_block, 2), along(down_block, -2))
        phonon[p, "b"] = (from_behind[p], from_ahead[p], swap(mixed))
        deps = [mixed]

    def do_slab(kind, t):
        nonlocal deps
        if kind == 0:
            head = (retarded_kernel, "retarded"), (ivec, fvec, levels), (coupling, hamilton), contact_r
        else:
            head = (lesser_kernel, "lesser"), (ivec, fvec), (coupling, ret_of[t]), contact_l
        (kernel, name), scalars, fixed, top_block = head
        send, state[kind] = slab_call(
            kernel, name, n, t, slabs, ne, where[kind], scalars, fixed,
            handed[kind].get(t - 2), top_block,
            phonon, state[kind], deps,
            retarded_scratch(n) if kind == 0 else lesser_scratch(n), 32,
        )
        if kind == 0:
            ret_of[t] = send
        handed[kind][t] = hand_on(send, t)
        deps = [send]

    for step in PLAN:
        if step == "c":
            contact_l = starting_lesser(n, ne, fvec, contact[0], deps)
            deps = [contact_l]
        elif step[0] == "w":
            do_lay_out(int(step[1:]))
        elif step[0] == "x":
            do_exchange(int(step[1:]))
        elif step[0] == "d":
            p, name = int(step[1]), step[2]
            deps = deps + list(phonon[p, name])[0 if name == "a" else 2 :]
        else:
            do_slab("rl".index(step[0]), int(step[1:]))

    shape = (1, ne, 1, 2, n, n)
    return state[0].reshape(shape), state[1].reshape(shape)


def solution(mesh):
    in_specs = (
        P(),
        P("kt", "slab", None),
        P("kt", "slab", None, None, None),
        P("kt", "slab", None, None, None),
        P("kt", None, None, None),
        P("kt", None, "slab", None, None, None, None),
        P("kt", None),
        P("kt", None),
        P(),
    )
    out_specs = (P("kt", None, "slab", None, None, None), P("kt", None, "slab", None, None, None))
    return jax.shard_map(body, mesh=mesh, in_specs=in_specs, out_specs=out_specs, check_vma=False)
```

```python
import functools

import jax
import jax.numpy as jnp
from jax import lax
from jax.experimental import pallas as pl
from jax.experimental.pallas import tpu as pltpu
from jax.sharding import PartitionSpec as P

broaden = 0.05
fermi_level = 0.0
thermal = 0.1

BF = jnp.bfloat16
F32 = jnp.float32
ANY = pl.BlockSpec(memory_space=pl.ANY)
SMEM = pl.BlockSpec(memory_space=pltpu.SMEM)
VMEM = pl.BlockSpec(memory_space=pltpu.VMEM)

A_SWAP, A_BEHIND, A_AHEAD = 0, 1, 2
B_BEHIND, B_AHEAD, B_SWAP = 3, 4, 5
EVEN = 6
ENERGY = 7
INFO = 16
NEAR_BEHIND, NEAR_AHEAD, MODE_BEHIND, MODE_AHEAD = 0, 1, 2, 3


def dot(a, b):
    return jnp.dot(a, b, preferred_element_type=F32)


def dot_nt(a, b):
    return lax.dot_general(a, b, (((1,), (1,)), ((), ())), preferred_element_type=F32)


def params(flops, nbytes):
    return dict(
        compiler_params=pltpu.CompilerParams(vmem_limit_bytes=24 * 1024 * 1024),
        cost_estimate=pl.CostEstimate(flops=flops, bytes_accessed=nbytes, transcendentals=0),
    )


def lay_out_kernel(blocks, with_info, n_dep, prev, *rest):
    info = rest[0] if with_info else None
    rest = rest[with_info + n_dep :]
    outs, buffers, sems = rest[: len(blocks)], rest[len(blocks) : 2 * len(blocks)], rest[-1]
    rows = prev.shape[2]
    loads, stores = [], []
    for i, (first, count, kind) in enumerate(blocks):
        loads.append(
            [
                pltpu.make_async_copy(
                    prev.at[first + e, kind], buffers[i].at[pl.ds(e * rows, rows)], sems.at[i, e]
                )
                for e in range(count)
            ]
        )
        for c in loads[-1]:
            c.start()
    for i, (first, count, kind) in enumerate(blocks):
        if with_info:
            buffers[i][count * rows :] = info[...]
        for c in loads[i]:
            c.wait()
        stores.append(pltpu.make_async_copy(buffers[i], outs[i], sems.at[i, 0]))
        stores[-1].start()
    for c in stores:
        c.wait()


def lay_out(n, number, blocks, prev, info, deps):
    shapes = [(b[1] * 2 * n + (0 if info is None else INFO), n) for b in blocks]
    most = max(b[1] for b in blocks)
    infos = [] if info is None else [info]
    return pl.pallas_call(
        functools.partial(lay_out_kernel, blocks, len(infos), len(deps)),
        out_shape=[jax.ShapeDtypeStruct(s, BF) for s in shapes],
        in_specs=[ANY] + [VMEM] * len(infos) + [ANY] * len(deps),
        out_specs=[ANY] * len(blocks),
        scratch_shapes=[pltpu.VMEM(s, BF) for s in shapes] + [pltpu.SemaphoreType.DMA((len(blocks), most))],
        name=f"lay_out_{number}",
        compiler_params=pltpu.CompilerParams(vmem_limit_bytes=60 * 1024 * 1024),
    )(prev, *infos, *deps)


def exchange_kernel(own_a, own_b, ne, modes, n_dep, fvec, prev, swapped, behind, ahead, info_s, info_b, info_a, *rest):
    up, down, mixed, own_v, beh_v, ahe_v, up_v, down_v, mix_v, info_v, sems = rest[n_dep:]
    rows = prev.shape[2]
    infos = []
    for i, r in enumerate((info_s, info_b, info_a)):
        c = pltpu.make_async_copy(r.at[pl.ds(r.shape[0] - INFO, INFO)], info_v.at[i], sems.at[7 + i])
        c.start()
        infos.append(c)
    loads = [
        pltpu.make_async_copy(prev.at[own_b[0] + e, own_b[2]], own_v.at[pl.ds(e * rows, rows)], sems.at[2])
        for e in range(own_b[1])
    ]
    loads += [
        pltpu.make_async_copy(r.at[pl.ds(0, own_b[1] * rows)], v, sems.at[3 + i])
        for i, (r, v) in enumerate(((behind, beh_v), (ahead, ahe_v)))
    ]
    for c in infos:
        c.wait()
    told = [info_v[i].astype(F32) for i in range(3)]

    def value(who, row):
        return jnp.max(told[who][row : row + 1, :])

    even = fvec[EVEN]
    take_up = even * value(2, NEAR_BEHIND)
    take_down = (1.0 - even) * value(1, NEAR_AHEAD)
    chosen = []
    for i, (flag, v, dst) in enumerate(((take_up, up_v, up), (take_down, down_v, down))):

        @pl.when(flag < 0.5)
        def _(i=i, v=v):
            for e in range(own_a[1]):
                pltpu.make_async_copy(
                    prev.at[own_a[0] + e, own_a[2]], v.at[pl.ds(e * rows, rows)], sems.at[i]
                ).start()

        @pl.when(flag >= 0.5)
        def _(i=i, v=v):
            pltpu.make_async_copy(swapped.at[pl.ds(0, own_a[1] * rows)], v, sems.at[i]).start()

        chosen.append((pltpu.make_async_copy(v, v, sems.at[i]), pltpu.make_async_copy(v, dst, sems.at[5 + i])))
    for c in loads:
        c.start()

    def strength(row):
        mode = value(0, row)
        picked = jnp.float32(0.0)
        for m in range(modes):
            picked = jnp.where(jnp.abs(mode - m) < 0.5, fvec[ENERGY + ne + m], picked)
        return picked

    want_behind = value(0, NEAR_BEHIND) * strength(MODE_BEHIND)
    want_ahead = value(0, NEAR_AHEAD) * strength(MODE_AHEAD)
    own_w = even * want_behind + (1.0 - even) * want_ahead
    behind_w = (1.0 - even) * want_behind
    ahead_w = even * want_ahead
    for load, store in chosen:
        load.wait()
        store.start()
    for c in loads:
        c.wait()
    for e in range(own_b[1]):
        r = slice(e * rows, (e + 1) * rows)
        mix_v[r] = (
            own_w * own_v[r].astype(F32)
            + behind_w * beh_v[r].astype(F32)
            + ahead_w * ahe_v[r].astype(F32)
        ).astype(BF)
    last = pltpu.make_async_copy(mix_v, mixed, sems.at[2])
    last.start()
    for _, store in chosen:
        store.wait()
    last.wait()


def exchange(n, number, own_a, own_b, ne, modes, fvec, prev, swapped, behind, ahead, infos, deps):
    a = (own_a[1] * 2 * n, n)
    b = (own_b[1] * 2 * n, n)
    return pl.pallas_call(
        functools.partial(exchange_kernel, own_a, own_b, ne, modes, len(deps)),
        out_shape=[jax.ShapeDtypeStruct(s, BF) for s in (a, a, b)],
        in_specs=[SMEM] + [ANY] * (7 + len(deps)),
        out_specs=[ANY] * 3,
        scratch_shapes=[pltpu.VMEM(s, BF) for s in (b, b, b, a, a, b)]
        + [pltpu.VMEM((3, INFO, n), BF), pltpu.SemaphoreType.DMA((10,))],
        name=f"exchange_{number}",
        **params(6 * n * n, 14 * n * n * 2),
    )(fvec, prev, swapped, behind, ahead, *infos, *deps)


def contact_kernel(ne, n_dep, fvec, contact, *rest):
    out = rest[n_dep]
    n = out.shape[-1]
    cr, ci = contact[0].astype(F32), contact[1].astype(F32)
    skew_r, skew_i = cr - cr.T, ci + ci.T
    for e in range(ne):
        energy = jnp.full((1, n), fvec[ENERGY + e], F32)
        minus = -1.0 / (1.0 + jnp.exp((energy - fermi_level) / thermal))
        out[e, :n] = (minus * skew_r).astype(BF)
        out[e, n:] = (minus * skew_i).astype(BF)


def starting_lesser(n, ne, fvec, contact, deps):
    return pl.pallas_call(
        functools.partial(contact_kernel, ne, len(deps)),
        out_shape=jax.ShapeDtypeStruct((ne, 2 * n, n), BF),
        in_specs=[SMEM, VMEM] + [ANY] * len(deps),
        out_specs=VMEM,
        name="contact",
        **params(20 * n * n, 12 * n * n * 2),
    )(fvec, contact, *deps)


def lag_of(slab, slabs):
    return 2 * (slabs - 1 - slab)


def slot_map(slot, slabs, energies):
    found = [(s, slot - lag_of(s, slabs)) for s in range(slabs)]
    return [(s, e) for s, e in found if 0 <= e < energies]


def fetch(pos, active, pieces):
    for s, _ in active:

        @pl.when(pos == s)
        def _(s=s):
            for source, dst, sem in pieces:
                pltpu.make_async_copy(source(s), dst, sem).start()


def fill(ref, n, low=True):
    ref[n:, :n] = -ref[:n, n:]
    if low:
        ref[n:, n:] = ref[:n, :n]


def put(ref, n, real, imaginary):
    ref[:n, :n] = real
    ref[:n, n:] = imaginary
    ref[n:, :n] = -imaginary
    ref[n:, n:] = real


def moved_and_self(n, crep, xrep, moved_v):
    fill(crep, n)
    fill(xrep, n)
    moved_v[...] = dot(crep[:n, :], xrep[...]).astype(BF)
    return dot_nt(moved_v[...], crep[...])


def weights_of(kind_of_block):
    return (A_SWAP, A_BEHIND, A_AHEAD) if kind_of_block == "a" else (B_BEHIND, B_AHEAD, B_SWAP)


def pick_weights(pos, fvec, active, where):
    picked = [jnp.float32(0.0)] * 3
    for s, e in active:
        names = weights_of(where[e][1])
        picked = [jnp.where(pos == s, fvec[0, w], p) for w, p in zip(names, picked)]
    return picked


def unpack(refs, n_fixed, wants, sources, n_skip):
    refs = list(refs)
    fixed, at = refs[:n_fixed], n_fixed
    boundaries = []
    for want in wants:
        boundaries.append(refs[at] if want else None)
        at += want
    groups = {}
    for g in sources:
        groups[g] = refs[at : at + 3]
        at += 3
    at += n_skip
    return fixed, boundaries, groups, refs[at], refs[at + 1], refs[at + 2 :]


def retarded_kernel(n, active, where, top, wants, sources, n_skip, *refs):
    pos = lax.axis_index("slab")
    fixed, (recv, contact), groups, send, state, scratch = unpack(refs, 4, wants, sources, n_skip)
    table, levels_h, coupling, hamilton_h = fixed
    (xrep, crep, h_v, p0_v, p1_v, p2_v, moved_v, wide_v, first_v, sys_v, frep, prep, out_v, onsite, fvec, sems) = scratch
    energy_of = dict(active)
    working = functools.reduce(jnp.logical_or, [pos == s for s, _ in active])

    def boundary(s):
        return contact if s == top else recv

    fetch(
        pos,
        active,
        parts_of(n, boundary, xrep, sems, 0)
        + parts_of(n, lambda s: coupling, crep, sems, 2)
        + [(lambda s: hamilton_h, h_v, sems.at[4])]
        + [(lambda s: table, fvec, sems.at[10]), (lambda s: levels_h, onsite, sems.at[11])]
        + phonon_of(n, groups, where, energy_of, (p0_v, p1_v, p2_v), sems, 5),
    )

    @pl.when(working)
    def _():
        def wait(dst, k):
            pltpu.make_async_copy(dst, dst, sems.at[k]).wait()

        wait(fvec, 10)
        wait(onsite, 11)
        energy = jnp.float32(0.0)
        for s, e in active:
            energy = jnp.where(pos == s, fvec[0, ENERGY + e], energy)
        w0, w1, w2 = pick_weights(pos, fvec, active, where)
        wait_parts(n, wait, crep, 2)
        wait_parts(n, wait, xrep, 0)
        selfs = moved_and_self(n, crep, xrep, moved_v)
        for k, v in enumerate((h_v, p0_v, p1_v, p2_v)):
            wait(v, 4 + k)
        taken = (
            w0 * p0_v[...].astype(F32) + w1 * p1_v[...].astype(F32) + w2 * p2_v[...].astype(F32)
        )
        taken = taken + h_v[...].astype(F32)
        wide_v[:, :n] = -(taken[:n] + selfs[:, :n])
        wide_v[:, n:] = -(taken[n:] + selfs[:, n:])
        levels = energy - onsite[...]
        size = 128 if n % 128 == 0 else n
        row = lax.broadcasted_iota(jnp.int32, (size, size), 0)
        col = lax.broadcasted_iota(jnp.int32, (size, size), 1)
        eye = row == col
        zero = jnp.zeros((size, size), F32)
        squares = [slice(i, i + size) for i in range(0, n, size)]
        diagonals = []
        for q in squares:
            p = slice(n + q.start, n + q.stop)
            dr = jnp.where(eye, wide_v[q, q] + levels[:, q], zero)
            di = jnp.where(eye, wide_v[q, p] + broaden, zero)
            wide_v[q, q] = jnp.where(eye, dr, wide_v[q, q])
            wide_v[q, p] = jnp.where(eye, di, wide_v[q, p])
            diagonals.append((dr, di))

        def reciprocal(axis):
            dr = jnp.concatenate([jnp.sum(d[0], axis=axis, keepdims=True) for d in diagonals], axis=1 - axis)
            di = jnp.concatenate([jnp.sum(d[1], axis=axis, keepdims=True) for d in diagonals], axis=1 - axis)
            modulus = dr * dr + di * di
            return dr / modulus, -di / modulus

        cr, ci = reciprocal(1)
        rr, ri = reciprocal(0)
        sr, si = wide_v[:, :n], wide_v[:, n:]
        sys_v[:, :n] = sr.astype(BF)
        sys_v[:, n:] = si.astype(BF)
        tr = cr * sr - ci * si
        ti = cr * si + ci * sr
        first_v[:, :n] = ti * ri - tr * rr
        first_v[:, n:] = -(tr * ri + ti * rr)
        for q in squares:
            p = slice(n + q.start, n + q.stop)
            first_v[q, q] = first_v[q, q] + jnp.where(eye, 2.0 * cr[q], zero)
            first_v[q, p] = first_v[q, p] + jnp.where(eye, 2.0 * ci[q], zero)
        put(frep, n, first_v[:, :n].astype(BF), first_v[:, n:].astype(BF))
        product = dot(sys_v[...], frep[...])
        put(prep, n, product[:, :n].astype(BF), product[:, n:].astype(BF))
        correction = dot(frep[:n, :], prep[...])
        out_v[:n] = (2.0 * first_v[:, :n] - correction[:, :n]).astype(BF)
        out_v[n:] = (2.0 * first_v[:, n:] - correction[:, n:]).astype(BF)
        pltpu.make_async_copy(out_v, send, sems.at[8]).start()

    for s, e in active:

        @pl.when(pos == s)
        def _(e=e):
            pltpu.make_async_copy(out_v, state.at[e], sems.at[9]).start()

    @pl.when(working)
    def _():
        pltpu.make_async_copy(out_v, send, sems.at[8]).wait()
        pltpu.make_async_copy(out_v, send, sems.at[9]).wait()


def lesser_kernel(n, active, where, top, wants, sources, n_skip, *refs):
    pos = lax.axis_index("slab")
    fixed, (recv, contact), groups, send, state, scratch = unpack(refs, 3, wants, sources, n_skip)
    table, coupling, ret_h = fixed
    (xrep, crep, p0_v, p1_v, p2_v, moved_v, rrep, srep, half_v, out_v, fvec, sems) = scratch
    energy_of = dict(active)
    working = functools.reduce(jnp.logical_or, [pos == s for s, _ in active])

    def boundary(s):
        return contact.at[energy_of[s]] if s == top else recv

    fetch(
        pos,
        active,
        parts_of(n, boundary, xrep, sems, 0)
        + parts_of(n, lambda s: coupling, crep, sems, 2)
        + parts_of(n, lambda s: ret_h, rrep, sems, 4)
        + [(lambda s: table, fvec, sems.at[11])]
        + phonon_of(n, groups, where, energy_of, (p0_v, p1_v, p2_v), sems, 6),
    )

    @pl.when(working)
    def _():
        def wait(dst, k):
            pltpu.make_async_copy(dst, dst, sems.at[k]).wait()

        wait(fvec, 11)
        w0, w1, w2 = pick_weights(pos, fvec, active, where)
        wait_parts(n, wait, crep, 2)
        wait_parts(n, wait, xrep, 0)
        selfs = moved_and_self(n, crep, xrep, moved_v)
        for k, v in enumerate((p0_v, p1_v, p2_v)):
            wait(v, 6 + k)
        taken = (
            w0 * p0_v[...].astype(F32) + w1 * p1_v[...].astype(F32) + w2 * p2_v[...].astype(F32)
        )
        put(srep, n, (taken[:n] + selfs[:, :n]).astype(BF), (taken[n:] + selfs[:, n:]).astype(BF))
        wait_parts(n, wait, rrep, 4)
        fill(rrep, n)
        half_v[...] = dot(rrep[:n, :], srep[...]).astype(BF)
        lesser = dot_nt(half_v[...], rrep[...])
        out_v[:n] = lesser[:, :n].astype(BF)
        out_v[n:] = lesser[:, n:].astype(BF)
        pltpu.make_async_copy(out_v, send, sems.at[9]).start()

    for s, e in active:

        @pl.when(pos == s)
        def _(e=e):
            pltpu.make_async_copy(out_v, state.at[e], sems.at[10]).start()

    @pl.when(working)
    def _():
        pltpu.make_async_copy(out_v, send, sems.at[9]).wait()
        pltpu.make_async_copy(out_v, send, sems.at[10]).wait()


def parts_of(n, source, rep, sems, at):
    return [
        (lambda s: source(s).at[:n], rep.at[:n, :n], sems.at[at]),
        (lambda s: source(s).at[n:], rep.at[:n, n:], sems.at[at + 1]),
    ]


def wait_parts(n, wait, rep, at):
    wait(rep.at[:n, :n], at)
    wait(rep.at[:n, n:], at + 1)


def phonon_of(n, groups, where, energy_of, buffers, sems, at):
    def source(i):
        def found(s):
            pair, block, inside = where[energy_of[s]]
            return groups[pair, block][i].at[pl.ds(inside * 2 * n, 2 * n)]

        return found

    return [(source(i), v, sems.at[at + i]) for i, v in enumerate(buffers)]


def slab_call(kernel, name, n, slot, slabs, energies, where, scalars, fixed, recv, top_block, phonon, state, deps, scratch, flops):
    active = slot_map(slot, slabs, energies)
    top = slabs - 1
    wants = (
        any(s != top for s, _ in active),
        any(s == top for s, _ in active),
    )
    sources = sorted({where[e][:2] for _, e in active})
    operands = list(scalars) + list(fixed)
    operands += [b for b, want in zip((recv, top_block), wants) if want]
    for g in sources:
        operands += list(phonon[g])
    aliases = {}
    if state is not None:
        aliases = {len(operands): 1}
        operands.append(state)
    operands += list(deps)
    block = jax.ShapeDtypeStruct((2 * n, n), BF)
    return pl.pallas_call(
        functools.partial(
            kernel, n, active, where, top, wants, sources, (state is not None) + len(deps)
        ),
        out_shape=[block, jax.ShapeDtypeStruct((energies, 2 * n, n), BF)],
        in_specs=[ANY] * len(operands),
        out_specs=[ANY, ANY],
        scratch_shapes=scratch,
        input_output_aliases=aliases,
        name=f"{name}_{slot}",
        **params(flops * n * n * n, 20 * n * n * 2),
    )(*operands)


def retarded_scratch(n):
    b = pltpu.VMEM((2 * n, n), BF)
    w = pltpu.VMEM((2 * n, 2 * n), BF)
    t = pltpu.VMEM((n, 2 * n), BF)
    f = pltpu.VMEM((n, 2 * n), F32)
    return [w, w, b, b, b, b, t, f, f, t, w, w, b, pltpu.VMEM((1, n), F32), pltpu.SMEM((1, 128), F32), pltpu.SemaphoreType.DMA((12,))]


def lesser_scratch(n):
    b = pltpu.VMEM((2 * n, n), BF)
    w = pltpu.VMEM((2 * n, 2 * n), BF)
    t = pltpu.VMEM((n, 2 * n), BF)
    return [w, w, b, b, b, t, w, w, t, b, pltpu.SMEM((1, 128), F32), pltpu.SemaphoreType.DMA((12,))]


def pairs_of(ne):
    half = ne // 2
    return [
        ((0, half, 0), (half, half, 0)),
        ((0, half, 1), (half, half, 1)),
    ]


PLAN = (
    "w0", "w1", "c", "x0", "x1", "d0b", "r0", "r1", "r2", "d1a", "d1b", "r3", "l0", "r4", "l1", "r5", "l2", "r6", "l3", "r7", "l4", "r8", "l5", "r9", "l6", "l7", "l8", "l9",
)


def body(energies, onsite, hamiltonian, hopping, contact, previous, neighbours, mode_index, mode_strength):
    slabs = lax.axis_size("slab")
    points = lax.axis_size("kt")
    k = lax.axis_index("kt")
    ne, n = previous.shape[1], previous.shape[-1]
    modes = mode_strength.shape[0]

    def along(value, shift):
        return lax.ppermute(value, "kt", [(i, (i + shift) % points) for i in range(points)])

    def swap(value):
        return lax.ppermute(value, "kt", [(i, i ^ 1) for i in range(points)])

    def hand_on(value, slot):
        senders = [s for s, _ in slot_map(slot, slabs, ne) if s > 0]
        return lax.ppermute(value, "slab", [(s, s - 1) for s in senders]) if senders else None

    pairs = pairs_of(ne)
    where = [{}, {}]
    for p, both in enumerate(pairs):
        for name, (first, count, kind) in zip("ab", both):
            for e in range(count):
                where[kind][first + e] = (p, name, e)
    prev = previous.reshape(ne, 2, 2 * n, n)

    strength = jnp.sum(
        jnp.where(mode_index[0][:, None] == jnp.arange(modes)[None, :], mode_strength[None, :], 0.0), axis=1
    )
    wanted = jnp.stack([(k - 1) % points, (k + 1) % points])
    near = (neighbours[0] == wanted).astype(F32)
    info = jnp.concatenate([near, mode_index[0].astype(F32), jnp.zeros((INFO - 4,), F32)])
    info = jnp.broadcast_to(info[:, None], (INFO, n)).astype(BF)
    even = (k % 2 == 0).astype(F32)
    odd = 1.0 - even
    far = 1.0 - near
    fvec = jnp.concatenate(
        [
            jnp.stack(
                [
                    even * near[1] * strength[1] + odd * near[0] * strength[0],
                    strength[0] * (even + odd * far[0]),
                    strength[1] * (odd + even * far[1]),
                    strength[0] * far[0],
                    strength[1] * far[1],
                    jnp.float32(1.0),
                    even,
                ]
            ),
            energies,
            mode_strength,
        ]
    )
    table = jnp.pad(fvec, (0, 128 - fvec.shape[0]))[None]
    coupling = hopping.reshape(2 * n, n)
    hamilton = hamiltonian.reshape(2 * n, n)
    contact_r = contact.reshape(2 * n, n)
    contact_l = None
    levels = onsite.reshape(1, n)

    swapped, from_behind, from_ahead = {}, {}, {}
    phonon = {}
    slots = ne + lag_of(0, slabs)
    state = [None, None]
    handed = [{}, {}]
    ret_of = {}
    deps = []

    def do_lay_out(p):
        nonlocal deps
        block_a, block_b = lay_out(n, p, pairs[p], prev, info if p == 0 else None, deps)
        swapped[p] = swap(block_a)
        from_behind[p] = along(block_b, 2)
        from_ahead[p] = along(block_b, -2)
        deps = [block_b]

    def do_exchange(p):
        nonlocal deps
        own_a, own_b = pairs[p]
        up_block, down_block, mixed = exchange(
            n, p, own_a, own_b, ne, modes, fvec, prev, swapped[p], from_behind[p], from_ahead[p],
            (swapped[0], from_behind[0], from_ahead[0]), deps,
        )
        phonon[p, "a"] = (swapped[p], along(up_block, 2), along(down_block, -2))
        phonon[p, "b"] = (from_behind[p], from_ahead[p], swap(mixed))
        deps = [mixed]

    def do_slab(kind, t):
        nonlocal deps
        if kind == 0:
            head = (retarded_kernel, "retarded"), (table, levels), (coupling, hamilton), contact_r
        else:
            head = (lesser_kernel, "lesser"), (table,), (coupling, ret_of[t]), contact_l
        (kernel, name), scalars, fixed, top_block = head
        send, state[kind] = slab_call(
            kernel, name, n, t, slabs, ne, where[kind], scalars, fixed,
            handed[kind].get(t - 2), top_block,
            phonon, state[kind], deps,
            retarded_scratch(n) if kind == 0 else lesser_scratch(n), 32,
        )
        if kind == 0:
            ret_of[t] = send
        handed[kind][t] = hand_on(send, t)
        deps = [send]

    for step in PLAN:
        if step == "c":
            contact_l = starting_lesser(n, ne, fvec, contact[0], deps)
            deps = [contact_l]
        elif step[0] == "w":
            do_lay_out(int(step[1:]))
        elif step[0] == "x":
            do_exchange(int(step[1:]))
        elif step[0] == "d":
            p, name = int(step[1]), step[2]
            deps = deps + list(phonon[p, name])[0 if name == "a" else 2 :]
        else:
            do_slab("rl".index(step[0]), int(step[1:]))

    shape = (1, ne, 1, 2, n, n)
    return state[0].reshape(shape), state[1].reshape(shape)


def solution(mesh):
    in_specs = (
        P(),
        P("kt", "slab", None),
        P("kt", "slab", None, None, None),
        P("kt", "slab", None, None, None),
        P("kt", None, None, None),
        P("kt", None, "slab", None, None, None, None),
        P("kt", None),
        P("kt", None),
        P(),
    )
    out_specs = (P("kt", None, "slab", None, None, None), P("kt", None, "slab", None, None, None))
    return jax.shard_map(body, mesh=mesh, in_specs=in_specs, out_specs=out_specs, check_vma=False)
```
